128 devices in a mesh: gx: 64 (over y, x, z_hi, core), ta: 2 (over z_lo).
Axes of the slice: x: 4, y: 4, z: 4 (z_hi: 2, z_lo: 2; z = z_hi * 2 + z_lo), core: 2. Of those that a mesh axis runs over, the one named last changes fastest.
Arguments:
- voltages: int32 [512, 524288], P('gx', 'ta'), may hold values from -128 to 127
Outputs:
- visibilities: float32 [1024, 2, 512, 512], P(('gx', 'ta'))
The draws below stay inside these ranges and needn't reach their ends.
All inputs are finite; a program needn't handle non-finite values.
Results may differ from the reference program's by a relative error of at most 0.0052.
Values may be sent and summed in bfloat16 or wider, within the bound.
No kernel may reach another device: no remote copies, remote signals or barrier semaphores. Data moves between devices by JAX's collectives and lax.ppermute only.
A program may use at most 192 MiB of HBM per device.

```python
import math
import jax
import jax.numpy as jnp
from jax import lax

INPUTS = 512
CHAN = 1024
TAPS = 4
SPECTRA = 256
SAMPLES = 524288


def set_ends(values, rng, low, largest):
    index_at = [jax.random.randint(jax.random.fold_in(rng, axis), (), 0, length) for axis, length in enumerate(values.shape)]
    main_axis = values.shape.index(max(values.shape))
    next_to = index_at[:main_axis] + [(index_at[main_axis] + 1) % values.shape[main_axis]] + index_at[main_axis + 1:]
    return values.at[tuple(index_at)].set(low).at[tuple(next_to)].set(largest)


def setup_inputs(seed: int = 0) -> dict:
    streams_of = jax.random.split(jax.random.key(seed), 2)
    voltages = set_ends(jax.random.randint(streams_of[0], (INPUTS, SAMPLES), -128, 128), jax.random.fold_in(streams_of[0], 1), -128, 127).astype(jnp.int32)
    return dict(voltages=voltages)


def window_taps(frame_len):
    total_len = TAPS * frame_len
    positions = jnp.arange(total_len, dtype=jnp.float32)
    centred = (positions + 0.5 - total_len / 2.0) / frame_len
    hamming = 0.54 - 0.46 * jnp.cos(2.0 * jnp.pi * positions / (total_len - 1))
    return (jnp.sinc(centred) * hamming).reshape(TAPS, frame_len)

def dft_rows(chan_list, frame_len):
    samples_index = jnp.arange(frame_len, dtype=jnp.int32)
    phase = chan_list[:, None] * samples_index[None, :] % frame_len
    angle = phase.astype(jnp.float32) * (2.0 * jnp.pi / frame_len)
    rows = jnp.stack([jnp.cos(angle), -jnp.sin(angle)], axis=1)
    return rows.reshape(2 * chan_list.shape[0], frame_len).astype(jnp.bfloat16)

def correlate(chan_block):
    stacked = chan_block.astype(jnp.float32)
    gram = jnp.einsum('cas,cbs->cab', stacked, stacked)
    real_part = gram[:, :INPUTS, :INPUTS] + gram[:, INPUTS:, INPUTS:]
    imag_part = gram[:, INPUTS:, :INPUTS] - gram[:, :INPUTS, INPUTS:]
    return jnp.stack([real_part, imag_part], axis=1) * (1.0 / math.sqrt(SPECTRA))

def reference(voltages):
    frame_len = 2 * CHAN
    values = voltages.astype(jnp.float32)
    padding = jnp.zeros((INPUTS, (TAPS - 1) * frame_len), jnp.float32)
    history = jnp.concatenate([padding, values], axis=1)
    frames = history.reshape(INPUTS, SPECTRA + TAPS - 1, frame_len)
    weights = window_taps(frame_len)
    filtered = weights[0] * frames[:, 0:SPECTRA, :]
    for tap in range(1, TAPS):
        filtered = filtered + weights[tap] * frames[:, tap:tap + SPECTRA, :]
    filtered = filtered.astype(jnp.bfloat16)
    dft_table = dft_rows(jnp.arange(CHAN, dtype=jnp.int32), frame_len)
    spectra = jnp.einsum('cf,isf->cis', dft_table.astype(jnp.float32), filtered.astype(jnp.float32))
    spectra = (spectra * (1.0 / (64.0 * math.sqrt(frame_len)))).astype(jnp.bfloat16)
    stacked = spectra.reshape(CHAN // 16, 16, 2 * INPUTS, SPECTRA)
    result = lax.map(correlate, stacked)
    return result.reshape(CHAN, 2, INPUTS, INPUTS)
```

```python
import math

import jax
import jax.numpy as jnp
import numpy as np
from jax import lax
from jax.experimental import pallas as pl
from jax.experimental.pallas import tpu as pltpu
from jax.sharding import PartitionSpec as P

INPUTS = 512
CHAN = 1024
TAPS = 4
FRAME = 2 * CHAN
HALF = FRAME // 2
LANES = 128
TILES = FRAME // LANES
HTILES = TILES // 2
HEAD = 16
MIB = 1024 * 1024
BF16 = jnp.bfloat16
F32 = jnp.float32


def shifted(array, axis, by):
    count = lax.axis_size(axis)
    pairs = [(i, i + by) for i in range(count) if 0 <= i + by < count]
    return lax.ppermute(array, axis, pairs)


def window_rows():
    total_len = TAPS * FRAME
    positions = np.arange(total_len, dtype=np.float64)
    centred = (positions + 0.5 - total_len / 2.0) / FRAME
    hamming = 0.54 - 0.46 * np.cos(2.0 * np.pi * positions / (total_len - 1))
    return (np.sinc(centred) * hamming).astype(np.float32).reshape(TAPS * TILES, LANES)


def dft_half(parity):
    chan = 2 * np.arange(CHAN // 2) + parity
    phase = chan[:, None] * np.arange(HALF)[None, :] % FRAME
    angle = phase * (2.0 * np.pi / FRAME)
    rows = np.stack([np.cos(angle), -np.sin(angle)], axis=1)
    return rows.reshape(CHAN, HALF).astype(BF16)


def taps_into(acc_ref, history, frame_at, weights, count, base=0):
    def step(block, carry):
        carry = list(carry)
        for inner in range(8):
            s = block * 8 + inner
            new = frame_at(s)
            total = weights[0] * carry[0] + weights[1] * carry[1]
            total = total + weights[2] * carry[2] + weights[3] * new
            acc_ref[pl.ds(pl.multiple_of(s * 8, 8), 8), :] = total
            carry = [carry[1], carry[2], new]
        return tuple(carry)

    lax.fori_loop(0, count // 8, step, tuple(history))


def fold_into(fe_ref, fo_ref, lo_ref, hi_ref, spec_here, count, column, inputs_here):
    lanes = pl.ds(pl.multiple_of(column * LANES, LANES), LANES)
    for i in range(inputs_here):
        for c in range(count // 16):
            rows = pl.ds(c * 16 * inputs_here + i, 16, stride=inputs_here)
            low = lo_ref[rows, :].astype(BF16)
            high = hi_ref[rows, :].astype(BF16)
            place = pl.ds(i * spec_here + c * 16, 16)
            fe_ref[place, lanes] = low + high
            fo_ref[place, lanes] = low - high


def window_at(w_ref, tile):
    return [jnp.broadcast_to(w_ref[pl.ds(t * TILES + tile, 1), :], (8, LANES)) for t in range(TAPS)]


def filter_kernel(spec_here, v_hbm, w_ref, fe_ref, fo_ref, lo_acc, hi_acc):
    def body(lo_ref, hi_ref):
        j = pl.program_id(0)
        for ref, acc, tile in ((lo_ref, lo_acc, j), (hi_ref, hi_acc, j + HTILES)):
            weights = window_at(w_ref, tile)
            zero = jnp.zeros((8, LANES), F32)
            taps_into(acc, [zero] * 3, lambda s: ref[s, 0].astype(F32), weights, spec_here)
        fold_into(fe_ref, fo_ref, lo_acc, hi_acc, spec_here, spec_here, j, 8)

    block = (spec_here, 1, 8, LANES)
    pltpu.emit_pipeline(
        body,
        grid=(HTILES,),
        in_specs=[
            pl.BlockSpec(block, lambda j: (0, j, 0, 0)),
            pl.BlockSpec(block, lambda j: (0, j + HTILES, 0, 0)),
        ],
        out_specs=[],
    )(v_hbm, v_hbm)


def dft_kernel(spec_here, head_ref, halo_ref, w_ref, te_ref, to_ref, fe_in, fo_in, out_ref, fe_ref, fo_ref, lo_acc, hi_acc, scr):
    def first(j, carry):
        for acc, tile in ((lo_acc, j), (hi_acc, j + HTILES)):
            weights = window_at(w_ref, tile)
            history = [halo_ref[t, tile].astype(F32) for t in range(TAPS - 1)]
            taps_into(acc, history, lambda s: head_ref[s, tile].astype(F32), weights, HEAD)
        fold_into(fe_ref, fo_ref, lo_acc, hi_acc, spec_here, HEAD, j, 8)
        return carry

    lax.fori_loop(0, HTILES, first, 0)
    scale = 1.0 / (64.0 * math.sqrt(FRAME))
    for parity, (table, data) in enumerate(((te_ref, fe_ref), (to_ref, fo_ref))):

        def pair(ip, carry):
            rhs = data[pl.ds(pl.multiple_of(ip * 2 * spec_here, 2 * spec_here), 2 * spec_here), :]
            for rc in range(2):
                lhs = table[rc * 512 : (rc + 1) * 512, :]
                acc = lax.dot_general(lhs, rhs, (((1,), (1,)), ((), ())), preferred_element_type=F32) * scale
                for side in range(2):
                    rows = pl.ds(rc * 512 * 8 + ip * 2 + side, 512, stride=8)
                    scr[rows, :] = acc[:, side * spec_here : (side + 1) * spec_here]
            return carry

        lax.fori_loop(0, 4, pair, 0)

        def emit(d, carry):
            rows = scr[pl.ds(pl.multiple_of(d * 256, 256), 256), :].astype(BF16)
            out_ref[pl.ds(d * 4, 4), pl.ds(parity * 64, 64), :] = rows.reshape(4, 64, LANES)
            return carry

        lax.fori_loop(0, 32, emit, 0)


def gram_kernel(norm, got_ref, out_hbm, mat):
    def body(out_ref):
        k = pl.program_id(0)
        row = pl.multiple_of((k % 2) * 64 + (k // 2) * 16, 16)
        for ta in range(2):
            tile = got_ref[:, ta, pl.ds(row, 16), :].astype(F32).reshape(64, 2, 8, LANES)
            real = tile[:, 0].reshape(INPUTS, LANES)
            imag = tile[:, 1].reshape(INPUTS, LANES)
            mat[:INPUTS, ta * 128 : (ta + 1) * 128] = real.astype(BF16)
            mat[:INPUTS, 256 + ta * 128 : 256 + (ta + 1) * 128] = imag.astype(BF16)
            mat[INPUTS:, ta * 128 : (ta + 1) * 128] = imag.astype(BF16)
            mat[INPUTS:, 256 + ta * 128 : 256 + (ta + 1) * 128] = (-real).astype(BF16)
        right = mat[:INPUTS, :]
        for p in range(2):
            left = mat[p * INPUTS : (p + 1) * INPUTS, :]
            gram = lax.dot_general(left, right, (((1,), (1,)), ((), ())), preferred_element_type=F32)
            out_ref[0, p] = gram * norm

    pltpu.emit_pipeline(
        body,
        grid=(8,),
        in_specs=[],
        out_specs=[pl.BlockSpec((1, 2, INPUTS, INPUTS), lambda k: (k, 0, 0, 0))],
    )(out_hbm)


VMEM = pl.BlockSpec(memory_space=pltpu.VMEM)
ANY = pl.BlockSpec(memory_space=pl.ANY)


def filter_call(frames, window):
    spec_here = frames.shape[0]
    rows = 8 * spec_here
    folded = jax.ShapeDtypeStruct((rows, HALF), BF16)
    return pl.pallas_call(
        lambda *refs: filter_kernel(spec_here, *refs),
        out_shape=(folded, folded),
        in_specs=[ANY, VMEM],
        out_specs=(VMEM, VMEM),
        scratch_shapes=[pltpu.VMEM((rows, LANES), F32)] * 2,
        compiler_params=pltpu.CompilerParams(vmem_limit_bytes=20 * MIB),
        cost_estimate=pl.CostEstimate(flops=8 * 2 * 1024 * 1024, bytes_accessed=8 * MIB, transcendentals=0),
        name="filter",
    )(frames, window)


def dft_call(head, halo, window, table_even, table_odd, even, odd):
    rows = even.shape[0]
    spec_here = rows // 8
    folded = jax.ShapeDtypeStruct((rows, HALF), BF16)
    return pl.pallas_call(
        lambda *refs: dft_kernel(spec_here, *refs),
        out_shape=(jax.ShapeDtypeStruct((128, 128, spec_here), BF16), folded, folded),
        in_specs=[VMEM] * 7,
        out_specs=(VMEM, VMEM, VMEM),
        input_output_aliases={5: 1, 6: 2},
        scratch_shapes=[pltpu.VMEM((HEAD * 8, LANES), F32)] * 2 + [pltpu.VMEM((8 * CHAN, spec_here), F32)],
        compiler_params=pltpu.CompilerParams(vmem_limit_bytes=40 * MIB),
        cost_estimate=pl.CostEstimate(flops=4 * 1024**3, bytes_accessed=12 * MIB, transcendentals=0),
        name="dft",
    )(head, halo, window, table_even, table_odd, even, odd)[0]


def gram_call(arrived, norm):
    return pl.pallas_call(
        lambda *refs: gram_kernel(norm, *refs),
        out_shape=jax.ShapeDtypeStruct((8, 2, INPUTS, INPUTS), F32),
        in_specs=[VMEM],
        out_specs=ANY,
        scratch_shapes=[pltpu.VMEM((2 * INPUTS, 512), BF16)],
        compiler_params=pltpu.CompilerParams(vmem_limit_bytes=20 * MIB),
        cost_estimate=pl.CostEstimate(flops=4 * 1024**3, bytes_accessed=20 * MIB, transcendentals=0),
        name="gram",
    )(arrived)


def on_device(voltages):
    inputs_here, total_len = voltages.shape
    spec_here = total_len // FRAME
    frames = voltages.reshape(inputs_here, spec_here, TILES, LANES).transpose(1, 2, 0, 3)
    tail = frames[spec_here - (TAPS - 1) :].astype(BF16)
    halo = shifted(tail, "ta", 1)
    window = jnp.asarray(window_rows())
    even, odd = filter_call(frames, window)
    table_even, table_odd = jnp.asarray(dft_half(0)), jnp.asarray(dft_half(1))
    outgoing = dft_call(frames[:HEAD], halo, window, table_even, table_odd, even, odd)
    arrived = lax.all_to_all(outgoing, ("gx", "ta"), split_axis=0, concat_axis=0, tiled=True)
    norm = 1.0 / math.sqrt(2 * spec_here)
    return gram_call(arrived.reshape(64, 2, 128, spec_here), norm)


def solution(mesh):
    placed = (P("gx", "ta"),)
    return jax.shard_map(
        on_device,
        mesh=mesh,
        in_specs=placed,
        out_specs=P(("gx", "ta"), None, None, None),
        check_vma=False,
    )
```

```python
import math

import jax
import jax.numpy as jnp
import numpy as np
from jax import lax
from jax.experimental import pallas as pl
from jax.experimental.pallas import tpu as pltpu
from jax.sharding import PartitionSpec as P

INPUTS = 512
CHAN = 1024
TAPS = 4
FRAME = 2 * CHAN
LANES = 128
TILES = FRAME // LANES
BLOCK = 16
MIB = 1024 * 1024
BF16 = jnp.bfloat16
F32 = jnp.float32


def shifted(array, axis, by):
    count = lax.axis_size(axis)
    pairs = [(i, i + by) for i in range(count) if 0 <= i + by < count]
    return lax.ppermute(array, axis, pairs)


def window_rows():
    total_len = TAPS * FRAME
    positions = np.arange(total_len, dtype=np.float64)
    centred = (positions + 0.5 - total_len / 2.0) / FRAME
    hamming = 0.54 - 0.46 * np.cos(2.0 * np.pi * positions / (total_len - 1))
    return (np.sinc(centred) * hamming).astype(np.float32).reshape(TAPS * TILES, LANES)


def dft_rows(first, step, length):
    chan = np.arange(first, CHAN, step)
    phase = chan[:, None] * np.arange(length)[None, :] % FRAME
    angle = phase * (2.0 * np.pi / FRAME)
    rows = np.stack([np.cos(angle), -np.sin(angle)], axis=1)
    return rows.reshape(2 * chan.size, length).astype(BF16)


def filter_block(frame_at, w_ref, acc_ref, f_ref, column, block, spec_here):
    for q in range(4):
        tile = column + 4 * q
        weights = [jnp.broadcast_to(w_ref[pl.ds(t * TILES + tile, 1), :], (8, LANES)) for t in range(TAPS)]
        frames = [frame_at(f, tile).astype(F32) for f in range(BLOCK + TAPS - 1)]
        for s in range(BLOCK):
            total = weights[0] * frames[s] + weights[1] * frames[s + 1]
            total = total + weights[2] * frames[s + 2] + weights[3] * frames[s + 3]
            acc_ref[q, s * 8 : (s + 1) * 8, :] = total
    for i in range(8):
        parts = [acc_ref[q, pl.ds(i, BLOCK, stride=8), :].astype(BF16) for q in range(4)]
        wide = [part.astype(F32) for part in parts]
        evens, odds = wide[0] + wide[2], wide[1] + wide[3]
        rows = pl.ds(pl.multiple_of(i * spec_here + block * BLOCK, BLOCK), BLOCK)
        f_ref[column, rows, :] = (evens + odds).astype(BF16)
        f_ref[4 + column, rows, :] = (evens - odds).astype(BF16)
        f_ref[8 + column, rows, :] = parts[0] - parts[2]
        f_ref[12 + column, rows, :] = parts[1] - parts[3]


def filter_kernel(spec_here, v_hbm, w_hbm, f_ref, head_ref, w_ref, frames, acc, sems, side_sems):
    blocks = spec_here // BLOCK

    def fetch(b):
        part = pl.ds(b * BLOCK, BLOCK)
        return pltpu.make_async_copy(v_hbm.at[part], frames.at[part], sems.at[b])

    window = pltpu.make_async_copy(w_hbm, w_ref, side_sems.at[0])
    window.start()
    for b in range(blocks):
        fetch(b).start()
    head = pltpu.make_async_copy(v_hbm.at[pl.ds(0, BLOCK)], head_ref, side_sems.at[1])
    head.start()
    window.wait()
    fetch(0).wait()

    def step(b, carry):
        fetch(b).wait()

        def columns(column, carry):
            filter_block(
                lambda f, tile: frames[b * BLOCK - (TAPS - 1) + f, tile], w_ref, acc, f_ref, column, b, spec_here
            )
            return carry

        return lax.fori_loop(0, 4, columns, carry)

    lax.fori_loop(1, blocks, step, 0)
    head.wait()


def dft_kernel(spec_here, head_ref, halo_ref, w_ref, t0_ref, t1_ref, t2_ref, f_in, out_ref, f_ref, acc, scr):
    def first(column, carry):
        def frame_at(f, tile):
            return halo_ref[f, tile] if f < TAPS - 1 else head_ref[f - (TAPS - 1), tile]

        filter_block(frame_at, w_ref, acc, f_ref, column, 0, spec_here)
        return carry

    lax.fori_loop(0, 4, first, 0)
    scale = 1.0 / (64.0 * math.sqrt(FRAME))
    pair = 2 * spec_here
    groups = ((t0_ref, 0, 0, 0, 32), (t1_ref, 4, 4096, 32, 32), (t2_ref, 8, 8192, 64, 64))
    for table, column, base, place, each in groups:
        rows_all, length = table.shape
        for ip in range(4):
            right = jnp.concatenate(
                [f_ref[column + c, ip * pair : (ip + 1) * pair, :] for c in range(length // LANES)], axis=1
            )
            for part in range(rows_all // 512):
                left = table[part * 512 : (part + 1) * 512, :]
                sums = lax.dot_general(left, right, (((1,), (1,)), ((), ())), preferred_element_type=F32) * scale
                for side in range(2):
                    rows = pl.ds(base + part * 4096 + ip * 2 + side, 512, stride=8)
                    scr[rows, :] = sums[:, side * spec_here : (side + 1) * spec_here]
        for d in range(0, 128, 4):
            rows = scr[base + d * each : base + (d + 4) * each, :].astype(BF16)
            out_ref[d : d + 4, place : place + each, :] = rows.reshape(4, each, LANES)


def gram_kernel(norm, got_ref, out_hbm, mats, out, sems):
    def copy_out(k, p):
        return pltpu.make_async_copy(out.at[k, p], out_hbm.at[k, p], sems.at[k, p])

    def channel(k, row, mat):
        for ta in range(2):
            tile = got_ref[:, ta, pl.ds(pl.multiple_of(row, 16), 16), :].astype(F32).reshape(64, 2, 8, LANES)
            real = tile[:, 0].reshape(INPUTS, LANES).astype(BF16)
            imag = tile[:, 1].reshape(INPUTS, LANES).astype(BF16)
            mat[:INPUTS, ta * 128 : (ta + 1) * 128] = real
            mat[:INPUTS, 256 + ta * 128 : 256 + (ta + 1) * 128] = imag
            mat[INPUTS:, ta * 128 : (ta + 1) * 128] = imag
            mat[INPUTS:, 256 + ta * 128 : 256 + (ta + 1) * 128] = -real
        for p in range(2):
            left = mat[p * INPUTS : (p + 1) * INPUTS, :]
            gram = lax.dot_general(left, mat[:INPUTS, :], (((1,), (1,)), ((), ())), preferred_element_type=F32)
            out[k, p] = gram * norm
            copy_out(k, p).start()

    def step(b, carry):
        channel(2 * b, (b % 2) * 32 + (b // 2) * 16, mats.at[0])
        channel(2 * b + 1, 64 + b * 16, mats.at[1])
        return carry

    lax.fori_loop(0, 4, step, 0)
    for k in range(8):
        for p in range(2):
            copy_out(k, p).wait()


VMEM = pl.BlockSpec(memory_space=pltpu.VMEM)
ANY = pl.BlockSpec(memory_space=pl.ANY)


def filter_call(frames, window):
    spec_here = frames.shape[0]
    return pl.pallas_call(
        lambda *refs: filter_kernel(spec_here, *refs),
        out_shape=(
            jax.ShapeDtypeStruct((TILES, 8 * spec_here, LANES), BF16),
            jax.ShapeDtypeStruct((BLOCK, TILES, 8, LANES), jnp.int32),
            window,
        ),
        in_specs=[ANY, ANY],
        out_specs=(VMEM, VMEM, VMEM),
        scratch_shapes=[
            pltpu.VMEM((spec_here, TILES, 8, LANES), jnp.int32),
            pltpu.VMEM((4, BLOCK * 8, LANES), F32),
            pltpu.SemaphoreType.DMA((spec_here // BLOCK,)),
            pltpu.SemaphoreType.DMA((2,)),
        ],
        compiler_params=pltpu.CompilerParams(vmem_limit_bytes=46 * MIB),
        cost_estimate=pl.CostEstimate(flops=8 * 2 * 1024 * 1024, bytes_accessed=8 * MIB, transcendentals=0),
        name="filter",
    )(frames, window)


def dft_call(head, halo, window, tables, folded):
    spec_here = folded.shape[1] // 8
    return pl.pallas_call(
        lambda *refs: dft_kernel(spec_here, *refs),
        out_shape=(jax.ShapeDtypeStruct((128, 128, spec_here), BF16), folded),
        in_specs=[VMEM] * 7,
        out_specs=(VMEM, VMEM),
        input_output_aliases={6: 1},
        scratch_shapes=[pltpu.VMEM((4, BLOCK * 8, LANES), F32), pltpu.VMEM((8 * FRAME, spec_here), F32)],
        compiler_params=pltpu.CompilerParams(vmem_limit_bytes=40 * MIB),
        cost_estimate=pl.CostEstimate(flops=3 * 1024**3, bytes_accessed=12 * MIB, transcendentals=0),
        name="dft",
    )(head, halo, window, *tables, folded)[0]


def gram_call(arrived, norm):
    return pl.pallas_call(
        lambda *refs: gram_kernel(norm, *refs),
        out_shape=jax.ShapeDtypeStruct((8, 2, INPUTS, INPUTS), F32),
        in_specs=[VMEM],
        out_specs=ANY,
        scratch_shapes=[
            pltpu.VMEM((2, 2 * INPUTS, 512), BF16),
            pltpu.VMEM((8, 2, INPUTS, INPUTS), F32),
            pltpu.SemaphoreType.DMA((8, 2)),
        ],
        compiler_params=pltpu.CompilerParams(vmem_limit_bytes=40 * MIB),
        cost_estimate=pl.CostEstimate(flops=4 * 1024**3, bytes_accessed=20 * MIB, transcendentals=0),
        name="gram",
    )(arrived)


def on_device(voltages):
    inputs_here, total_len = voltages.shape
    spec_here = total_len // FRAME
    frames = voltages.reshape(inputs_here, spec_here, TILES, LANES).transpose(1, 2, 0, 3)
    tail = frames[spec_here - (TAPS - 1) :].astype(BF16)
    halo = shifted(tail, "ta", 1)
    window = jnp.asarray(window_rows())
    folded, head, window = filter_call(frames, window)
    tables = [jnp.asarray(dft_rows(0, 4, 512)), jnp.asarray(dft_rows(2, 4, 512)), jnp.asarray(dft_rows(1, 2, 1024))]
    outgoing = dft_call(head, halo, window, tables, folded)
    arrived = lax.all_to_all(outgoing, ("gx", "ta"), split_axis=0, concat_axis=0, tiled=True)
    norm = 1.0 / math.sqrt(2 * spec_here)
    return gram_call(arrived.reshape(64, 2, 128, spec_here), norm)


def solution(mesh):
    placed = (P("gx", "ta"),)
    return jax.shard_map(
        on_device,
        mesh=mesh,
        in_specs=placed,
        out_specs=P(("gx", "ta"), None, None, None),
        check_vma=False,
    )
```

```python
import math

import jax
import jax.numpy as jnp
import numpy as np
from jax import lax
from jax.experimental import pallas as pl
from jax.experimental.pallas import tpu as pltpu
from jax.sharding import PartitionSpec as P

INPUTS = 512
CHAN = 1024
TAPS = 4
FRAME = 2 * CHAN
LANES = 128
TILES = FRAME // LANES
BLOCK = 16
MIB = 1024 * 1024
BF16 = jnp.bfloat16
F32 = jnp.float32


def halo_of(tail):
    count = lax.axis_size("ta")
    tail = jnp.where(lax.axis_index("ta") == count - 1, 0, tail).astype(BF16)
    return lax.ppermute(tail, "ta", [(i, (i + 1) % count) for i in range(count)])


def window_rows():
    total_len = TAPS * FRAME
    tile = lax.broadcasted_iota(jnp.int32, (TAPS * TILES, LANES), 0)
    lane = lax.broadcasted_iota(jnp.int32, (TAPS * TILES, LANES), 1)
    positions = (tile * LANES + lane).astype(F32)
    centred = (positions + 0.5 - total_len / 2.0) / FRAME
    hamming = 0.54 - 0.46 * jnp.cos(2.0 * jnp.pi * positions / (total_len - 1))
    return jnp.sinc(centred) * hamming


def dft_rows(first, step, length):
    chan = np.arange(first, CHAN, step)
    phase = chan[:, None] * np.arange(length)[None, :] % FRAME
    angle = phase * (2.0 * np.pi / FRAME)
    rows = np.stack([np.cos(angle), -np.sin(angle)], axis=1)
    return rows.reshape(2 * chan.size, length).astype(BF16)


def filter_block(frame_at, w_ref, acc_ref, f_ref, column, block, spec_here):
    for q in range(4):
        tile = column + 4 * q
        weights = [jnp.broadcast_to(w_ref[pl.ds(t * TILES + tile, 1), :], (8, LANES)) for t in range(TAPS)]
        frames = [frame_at(f, tile).astype(F32) for f in range(BLOCK + TAPS - 1)]
        for s in range(BLOCK):
            total = weights[0] * frames[s] + weights[1] * frames[s + 1]
            total = total + weights[2] * frames[s + 2] + weights[3] * frames[s + 3]
            acc_ref[q, s * 8 : (s + 1) * 8, :] = total
    for i in range(8):
        parts = [acc_ref[q, pl.ds(i, BLOCK, stride=8), :].astype(BF16) for q in range(4)]
        wide = [part.astype(F32) for part in parts]
        evens, odds = wide[0] + wide[2], wide[1] + wide[3]
        rows = pl.ds(pl.multiple_of(i * spec_here + block * BLOCK, BLOCK), BLOCK)
        f_ref[column, rows, :] = (evens + odds).astype(BF16)
        f_ref[4 + column, rows, :] = (evens - odds).astype(BF16)
        f_ref[8 + column, rows, :] = parts[0] - parts[2]
        f_ref[12 + column, rows, :] = parts[1] - parts[3]


def filter_kernel(spec_here, v_hbm, w_ref, f_ref, head_ref, frames, acc, sems, head_sem):
    blocks = spec_here // BLOCK

    def fetch(b):
        part = pl.ds(b * BLOCK, BLOCK)
        return pltpu.make_async_copy(v_hbm.at[part], frames.at[part], sems.at[b])

    for b in range(blocks):
        fetch(b).start()
    head = pltpu.make_async_copy(frames.at[pl.ds(0, BLOCK)], head_ref, head_sem)
    fetch(0).wait()
    head.start()

    def step(b, carry):
        fetch(b).wait()

        def columns(column, carry):
            filter_block(
                lambda f, tile: frames[b * BLOCK - (TAPS - 1) + f, tile], w_ref, acc, f_ref, column, b, spec_here
            )
            return carry

        return lax.fori_loop(0, 4, columns, carry)

    lax.fori_loop(1, blocks, step, 0)
    head.wait()


def dft_kernel(spec_here, head_ref, halo_ref, w_ref, t0_ref, t1_ref, t2_ref, f_in, out_ref, f_ref, acc, scr):
    def first(column, carry):
        def frame_at(f, tile):
            return halo_ref[f, tile] if f < TAPS - 1 else head_ref[f - (TAPS - 1), tile]

        filter_block(frame_at, w_ref, acc, f_ref, column, 0, spec_here)
        return carry

    lax.fori_loop(0, 4, first, 0)
    scale = 1.0 / (64.0 * math.sqrt(FRAME))
    pair = 2 * spec_here
    groups = ((t0_ref, 0, 0, 0, 32), (t1_ref, 4, 4096, 32, 32), (t2_ref, 8, 8192, 64, 64))
    for table, column, base, place, each in groups:
        rows_all, length = table.shape
        for ip in range(4):
            right = jnp.concatenate(
                [f_ref[column + c, ip * pair : (ip + 1) * pair, :] for c in range(length // LANES)], axis=1
            )
            for part in range(rows_all // 512):
                left = table[part * 512 : (part + 1) * 512, :]
                sums = lax.dot_general(left, right, (((1,), (1,)), ((), ())), preferred_element_type=F32) * scale
                for side in range(2):
                    rows = pl.ds(base + part * 4096 + ip * 2 + side, 512, stride=8)
                    scr[rows, :] = sums[:, side * spec_here : (side + 1) * spec_here]
        for d in range(0, 128, 4):
            rows = scr[base + d * each : base + (d + 4) * each, :].astype(BF16)
            out_ref[d : d + 4, place : place + each, :] = rows.reshape(4, each, LANES)


def gram_kernel(norm, got_ref, out_hbm, mats, out, sems):
    def copy_out(k, p):
        return pltpu.make_async_copy(out.at[k, p], out_hbm.at[k, p], sems.at[k, p])

    def channel(k, row, mat):
        for ta in range(2):
            tile = got_ref[:, ta, pl.ds(pl.multiple_of(row, 16), 16), :].astype(F32).reshape(64, 2, 8, LANES)
            real = tile[:, 0].reshape(INPUTS, LANES).astype(BF16)
            imag = tile[:, 1].reshape(INPUTS, LANES).astype(BF16)
            mat[:INPUTS, ta * 128 : (ta + 1) * 128] = real
            mat[:INPUTS, 256 + ta * 128 : 256 + (ta + 1) * 128] = imag
            mat[INPUTS:, ta * 128 : (ta + 1) * 128] = imag
            mat[INPUTS:, 256 + ta * 128 : 256 + (ta + 1) * 128] = -real
        for p in range(2):
            left = mat[p * INPUTS : (p + 1) * INPUTS, :]
            gram = lax.dot_general(left, mat[:INPUTS, :], (((1,), (1,)), ((), ())), preferred_element_type=F32)
            out[k, p] = gram * norm
            copy_out(k, p).start()

    def step(b, carry):
        channel(2 * b, (b % 2) * 32 + (b // 2) * 16, mats.at[0])
        channel(2 * b + 1, 64 + b * 16, mats.at[1])
        return carry

    lax.fori_loop(0, 4, step, 0)
    for k in range(8):
        for p in range(2):
            copy_out(k, p).wait()


VMEM = pl.BlockSpec(memory_space=pltpu.VMEM)
ANY = pl.BlockSpec(memory_space=pl.ANY)


def filter_call(frames, window):
    spec_here = frames.shape[0]
    return pl.pallas_call(
        lambda *refs: filter_kernel(spec_here, *refs),
        out_shape=(
            jax.ShapeDtypeStruct((TILES, 8 * spec_here, LANES), BF16),
            jax.ShapeDtypeStruct((BLOCK, TILES, 8, LANES), jnp.int32),
        ),
        in_specs=[ANY, VMEM],
        out_specs=(VMEM, VMEM),
        scratch_shapes=[
            pltpu.VMEM((spec_here, TILES, 8, LANES), jnp.int32),
            pltpu.VMEM((4, BLOCK * 8, LANES), F32),
            pltpu.SemaphoreType.DMA((spec_here // BLOCK,)),
            pltpu.SemaphoreType.DMA,
        ],
        compiler_params=pltpu.CompilerParams(vmem_limit_bytes=46 * MIB),
        cost_estimate=pl.CostEstimate(flops=8 * 2 * 1024 * 1024, bytes_accessed=8 * MIB, transcendentals=0),
        name="filter",
    )(frames, window)


def dft_call(head, halo, window, tables, folded):
    spec_here = folded.shape[1] // 8
    return pl.pallas_call(
        lambda *refs: dft_kernel(spec_here, *refs),
        out_shape=(jax.ShapeDtypeStruct((128, 128, spec_here), BF16), folded),
        in_specs=[VMEM] * 7,
        out_specs=(VMEM, VMEM),
        input_output_aliases={6: 1},
        scratch_shapes=[pltpu.VMEM((4, BLOCK * 8, LANES), F32), pltpu.VMEM((8 * FRAME, spec_here), F32)],
        compiler_params=pltpu.CompilerParams(vmem_limit_bytes=40 * MIB),
        cost_estimate=pl.CostEstimate(flops=3 * 1024**3, bytes_accessed=12 * MIB, transcendentals=0),
        name="dft",
    )(head, halo, window, *tables, folded)[0]


def gram_call(arrived, norm):
    return pl.pallas_call(
        lambda *refs: gram_kernel(norm, *refs),
        out_shape=jax.ShapeDtypeStruct((8, 2, INPUTS, INPUTS), F32),
        in_specs=[VMEM],
        out_specs=ANY,
        scratch_shapes=[
            pltpu.VMEM((2, 2 * INPUTS, 512), BF16),
            pltpu.VMEM((8, 2, INPUTS, INPUTS), F32),
            pltpu.SemaphoreType.DMA((8, 2)),
        ],
        compiler_params=pltpu.CompilerParams(vmem_limit_bytes=40 * MIB),
        cost_estimate=pl.CostEstimate(flops=4 * 1024**3, bytes_accessed=20 * MIB, transcendentals=0),
        name="gram",
    )(arrived)


def on_device(voltages):
    inputs_here, total_len = voltages.shape
    spec_here = total_len // FRAME
    frames = voltages.reshape(inputs_here, spec_here, TILES, LANES).transpose(1, 2, 0, 3)
    halo = halo_of(frames[spec_here - (TAPS - 1) :])
    window = window_rows()
    folded, head = filter_call(frames, window)
    tables = [jnp.asarray(dft_rows(0, 4, 512)), jnp.asarray(dft_rows(2, 4, 512)), jnp.asarray(dft_rows(1, 2, 1024))]
    outgoing = dft_call(head, halo, window, tables, folded)
    arrived = lax.all_to_all(outgoing, ("gx", "ta"), split_axis=0, concat_axis=0, tiled=True)
    norm = 1.0 / math.sqrt(2 * spec_here)
    return gram_call(arrived.reshape(64, 2, 128, spec_here), norm)


def solution(mesh):
    placed = (P("gx", "ta"),)
    return jax.shard_map(
        on_device,
        mesh=mesh,
        in_specs=placed,
        out_specs=P(("gx", "ta"), None, None, None),
        check_vma=False,
    )
```

```python
import math

import jax
import jax.numpy as jnp
import numpy as np
from jax import lax
from jax.experimental import pallas as pl
from jax.experimental.pallas import tpu as pltpu
from jax.sharding import PartitionSpec as P

INPUTS = 512
CHAN = 1024
TAPS = 4
FRAME = 2 * CHAN
LANES = 128
TILES = FRAME // LANES
BLOCK = 16
MIB = 1024 * 1024
BF16 = jnp.bfloat16
F32 = jnp.float32


def halo_of(tail):
    count = lax.axis_size("ta")
    tail = jnp.where(lax.axis_index("ta") == count - 1, 0, tail).astype(BF16)
    return lax.ppermute(tail, "ta", [(i, (i + 1) % count) for i in range(count)])


def window_rows():
    total_len = TAPS * FRAME
    tile = lax.broadcasted_iota(jnp.int32, (TAPS * TILES, LANES), 0)
    lane = lax.broadcasted_iota(jnp.int32, (TAPS * TILES, LANES), 1)
    positions = (tile * LANES + lane).astype(F32)
    centred = (positions + 0.5 - total_len / 2.0) / FRAME
    hamming = 0.54 - 0.46 * jnp.cos(2.0 * jnp.pi * positions / (total_len - 1))
    return jnp.sinc(centred) * hamming


def dft_rows(first, step, length):
    chan = np.arange(first, CHAN, step)
    phase = chan[:, None] * np.arange(length)[None, :] % FRAME
    angle = phase * (2.0 * np.pi / FRAME)
    rows = np.stack([np.cos(angle), -np.sin(angle)], axis=1)
    return rows.reshape(2 * chan.size, length).astype(BF16)


def filter_taps(frame_at, w_ref, acc_ref, column, q):
    tile = column + 4 * q
    weights = [jnp.broadcast_to(w_ref[pl.ds(t * TILES + tile, 1), :], (8, LANES)) for t in range(TAPS)]
    frames = [frame_at(f, tile).astype(F32) for f in range(BLOCK + TAPS - 1)]
    for s in range(BLOCK):
        total = weights[0] * frames[s] + weights[1] * frames[s + 1]
        total = total + weights[2] * frames[s + 2] + weights[3] * frames[s + 3]
        acc_ref[q, s * 8 : (s + 1) * 8, :] = total


def filter_fold(acc_ref, f_ref, column, block, spec_here, inputs):
    for i in inputs:
        parts = [acc_ref[q, pl.ds(i, BLOCK, stride=8), :].astype(BF16) for q in range(4)]
        wide = [part.astype(F32) for part in parts]
        evens, odds = wide[0] + wide[2], wide[1] + wide[3]
        rows = pl.ds(pl.multiple_of(i * spec_here + block * BLOCK, BLOCK), BLOCK)
        f_ref[column, rows, :] = (evens + odds).astype(BF16)
        f_ref[4 + column, rows, :] = (evens - odds).astype(BF16)
        f_ref[8 + column, rows, :] = parts[0] - parts[2]
        f_ref[12 + column, rows, :] = parts[1] - parts[3]


def filter_block(frame_at, w_ref, acc_ref, f_ref, column, block, spec_here):
    for q in range(4):
        filter_taps(frame_at, w_ref, acc_ref, column, q)
    filter_fold(acc_ref, f_ref, column, block, spec_here, range(8))


def filter_kernel(spec_here, v_hbm, w_ref, f_ref, head_ref, frames, acc_even, acc_odd, sems, head_sem):
    blocks = spec_here // BLOCK
    accs = (acc_even, acc_odd)

    def fetch(b):
        part = pl.ds(b * BLOCK, BLOCK)
        return pltpu.make_async_copy(v_hbm.at[part], frames.at[part], sems.at[b])

    first = pltpu.make_async_copy(v_hbm.at[pl.ds(BLOCK - 3, 3)], frames.at[pl.ds(BLOCK - 3, 3)], sems.at[0])
    first.start()
    for b in range(1, blocks):
        fetch(b).start()
    head = pltpu.make_async_copy(v_hbm.at[pl.ds(0, BLOCK)], head_ref, head_sem)
    head.start()
    first.wait()

    def step(b, carry):
        fetch(b).wait()

        def frame_at(f, tile):
            return frames[b * BLOCK - (TAPS - 1) + f, tile]

        for column in range(5):
            for q in range(4):
                if column < 4:
                    filter_taps(frame_at, w_ref, accs[column % 2], column, q)
                if column > 0:
                    filter_fold(accs[(column - 1) % 2], f_ref, column - 1, b, spec_here, range(2 * q, 2 * q + 2))
        return carry

    lax.fori_loop(1, blocks, step, 0)
    head.wait()


def dft_kernel(spec_here, head_ref, halo_ref, w_ref, t0_ref, t1_ref, t2_ref, f_in, out_ref, f_ref, acc, *results):
    def first(column, carry):
        def frame_at(f, tile):
            return halo_ref[f, tile] if f < TAPS - 1 else head_ref[f - (TAPS - 1), tile]

        filter_block(frame_at, w_ref, acc, f_ref, column, 0, spec_here)
        return carry

    lax.fori_loop(0, 4, first, 0)
    scale = 1.0 / (64.0 * math.sqrt(FRAME))
    pair = 2 * spec_here
    tasks = [
        (t2_ref, 0, 8, results[0], 64, 64, 0),
        (t2_ref, 512, 8, results[1], 64, 64, 64),
        (t0_ref, 0, 0, results[2], 0, 32, 0),
        (t1_ref, 0, 4, results[3], 32, 32, 0),
    ]

    def multiply(task, ip):
        table, first_row, column, result = task[:4]
        length = table.shape[1]
        right = jnp.concatenate(
            [f_ref[column + c, ip * pair : (ip + 1) * pair, :] for c in range(length // LANES)], axis=1
        )
        left = table[first_row : first_row + 512, :]
        sums = lax.dot_general(left, right, (((1,), (1,)), ((), ())), preferred_element_type=F32) * scale
        for side in range(2):
            result[pl.ds(ip * 2 + side, 512, stride=9), :] = sums[:, side * spec_here : (side + 1) * spec_here]

    def emit(task, quarter):
        result, place, each, start = task[3:]
        count = 4096 // each // 4
        for d in range(quarter * count, (quarter + 1) * count, 4):
            rows = [result[r * 9 : r * 9 + 8, :] for r in range(d * each // 8, (d + 4) * each // 8)]
            rows = jnp.concatenate(rows, axis=0).astype(BF16)
            out_ref[start + d : start + d + 4, place : place + each, :] = rows.reshape(4, each, LANES)

    for n in range(len(tasks) + 1):
        for quarter in range(4):
            if n < len(tasks):
                multiply(tasks[n], quarter)
            if n > 0:
                emit(tasks[n - 1], quarter)


def gram_kernel(norm, got_ref, out_hbm, mats, out, sems):
    def copy_out(k, p):
        return pltpu.make_async_copy(out.at[k, p], out_hbm.at[k, p], sems.at[k, p])

    def channel(k, row, mat):
        for ta in range(2):
            tile = got_ref[:, ta, pl.ds(pl.multiple_of(row, 16), 16), :].astype(F32).reshape(64, 2, 8, LANES)
            real = tile[:, 0].reshape(INPUTS, LANES).astype(BF16)
            imag = tile[:, 1].reshape(INPUTS, LANES).astype(BF16)
            mat[:INPUTS, ta * 128 : (ta + 1) * 128] = real
            mat[:INPUTS, 256 + ta * 128 : 256 + (ta + 1) * 128] = imag
            mat[INPUTS:, ta * 128 : (ta + 1) * 128] = imag
            mat[INPUTS:, 256 + ta * 128 : 256 + (ta + 1) * 128] = -real
        for p in range(2):
            left = mat[p * INPUTS : (p + 1) * INPUTS, :]
            gram = lax.dot_general(left, mat[:INPUTS, :], (((1,), (1,)), ((), ())), preferred_element_type=F32)
            out[k, p] = gram * norm
            copy_out(k, p).start()

    def step(b, carry):
        channel(2 * b, (b % 2) * 32 + (b // 2) * 16, mats.at[0])
        channel(2 * b + 1, 64 + b * 16, mats.at[1])
        return carry

    lax.fori_loop(0, 4, step, 0)
    for k in range(8):
        for p in range(2):
            copy_out(k, p).wait()


VMEM = pl.BlockSpec(memory_space=pltpu.VMEM)
ANY = pl.BlockSpec(memory_space=pl.ANY)


def filter_call(frames, window):
    spec_here = frames.shape[0]
    return pl.pallas_call(
        lambda *refs: filter_kernel(spec_here, *refs),
        out_shape=(
            jax.ShapeDtypeStruct((TILES, 8 * spec_here, LANES), BF16),
            jax.ShapeDtypeStruct((BLOCK, TILES, 8, LANES), jnp.int32),
        ),
        in_specs=[ANY, VMEM],
        out_specs=(VMEM, VMEM),
        scratch_shapes=[
            pltpu.VMEM((spec_here, TILES, 8, LANES), jnp.int32),
            pltpu.VMEM((4, BLOCK * 8, LANES), F32),
            pltpu.VMEM((4, BLOCK * 8, LANES), F32),
            pltpu.SemaphoreType.DMA((spec_here // BLOCK,)),
            pltpu.SemaphoreType.DMA,
        ],
        compiler_params=pltpu.CompilerParams(vmem_limit_bytes=46 * MIB),
        cost_estimate=pl.CostEstimate(flops=8 * 2 * 1024 * 1024, bytes_accessed=8 * MIB, transcendentals=0),
        name="filter",
    )(frames, window)


def dft_call(head, halo, window, tables, folded):
    spec_here = folded.shape[1] // 8
    return pl.pallas_call(
        lambda *refs: dft_kernel(spec_here, *refs),
        out_shape=(jax.ShapeDtypeStruct((128, 128, spec_here), BF16), folded),
        in_specs=[VMEM] * 7,
        out_specs=(VMEM, VMEM),
        input_output_aliases={6: 1},
        scratch_shapes=[pltpu.VMEM((4, BLOCK * 8, LANES), F32)] + [pltpu.VMEM((9 * 512, spec_here), F32)] * 4,
        compiler_params=pltpu.CompilerParams(vmem_limit_bytes=40 * MIB),
        cost_estimate=pl.CostEstimate(flops=3 * 1024**3, bytes_accessed=12 * MIB, transcendentals=0),
        name="dft",
    )(head, halo, window, *tables, folded)[0]


def gram_call(arrived, norm):
    return pl.pallas_call(
        lambda *refs: gram_kernel(norm, *refs),
        out_shape=jax.ShapeDtypeStruct((8, 2, INPUTS, INPUTS), F32),
        in_specs=[VMEM],
        out_specs=ANY,
        scratch_shapes=[
            pltpu.VMEM((2, 2 * INPUTS, 512), BF16),
            pltpu.VMEM((8, 2, INPUTS, INPUTS), F32),
            pltpu.SemaphoreType.DMA((8, 2)),
        ],
        compiler_params=pltpu.CompilerParams(vmem_limit_bytes=40 * MIB),
        cost_estimate=pl.CostEstimate(flops=4 * 1024**3, bytes_accessed=20 * MIB, transcendentals=0),
        name="gram",
    )(arrived)


def on_device(voltages):
    inputs_here, total_len = voltages.shape
    spec_here = total_len // FRAME
    frames = voltages.reshape(inputs_here, spec_here, TILES, LANES).transpose(1, 2, 0, 3)
    halo = halo_of(frames[spec_here - (TAPS - 1) :])
    window = window_rows()
    folded, head = filter_call(frames, window)
    tables = [jnp.asarray(dft_rows(0, 4, 512)), jnp.asarray(dft_rows(2, 4, 512)), jnp.asarray(dft_rows(1, 2, 1024))]
    outgoing = dft_call(head, halo, window, tables, folded)
    arrived = lax.all_to_all(outgoing, ("gx", "ta"), split_axis=0, concat_axis=0, tiled=True)
    norm = 1.0 / math.sqrt(2 * spec_here)
    return gram_call(arrived.reshape(64, 2, 128, spec_here), norm)


def solution(mesh):
    placed = (P("gx", "ta"),)
    return jax.shard_map(
        on_device,
        mesh=mesh,
        in_specs=placed,
        out_specs=P(("gx", "ta"), None, None, None),
        check_vma=False,
    )
```

```python
import functools
import math

import jax
import jax.numpy as jnp
import numpy as np
from jax import lax
from jax.experimental import pallas as pl
from jax.experimental.pallas import tpu as pltpu
from jax.sharding import PartitionSpec as P

INPUTS = 512
CHAN = 1024
TAPS = 4
FRAME = 2 * CHAN
LANES = 128
TILES = FRAME // LANES
BLOCK = 16
HALF = 64
MIB = 1024 * 1024
BF16 = jnp.bfloat16
F32 = jnp.float32


def halo_of(tail):
    count = lax.axis_size("ta")
    return lax.ppermute(tail, "ta", [(i, (i + 1) % count) for i in range(count)])


def window_rows():
    total_len = TAPS * FRAME
    tile = lax.broadcasted_iota(jnp.int32, (TAPS * TILES, LANES), 0)
    lane = lax.broadcasted_iota(jnp.int32, (TAPS * TILES, LANES), 1)
    positions = (tile * LANES + lane).astype(F32)
    centred = (positions + 0.5 - total_len / 2.0) / FRAME
    hamming = 0.54 - 0.46 * jnp.cos(2.0 * jnp.pi * positions / (total_len - 1))
    return jnp.sinc(centred) * hamming


def dft_rows(first, step, length):
    chan = np.arange(first, CHAN, step)
    phase = chan[:, None] * np.arange(length)[None, :] % FRAME
    angle = phase * (2.0 * np.pi / FRAME)
    rows = np.stack([np.cos(angle), -np.sin(angle)], axis=1)
    return rows.reshape(2 * chan.size, length).astype(BF16)


def filter_taps(frame_at, w_ref, acc_ref, column, q):
    tile = column + 4 * q
    weights = [jnp.broadcast_to(w_ref[pl.ds(t * TILES + tile, 1), :], (8, LANES)) for t in range(TAPS)]
    frames = [frame_at(f, tile).astype(F32) for f in range(BLOCK + TAPS - 1)]
    for s in range(BLOCK):
        total = weights[0] * frames[s] + weights[1] * frames[s + 1]
        total = total + weights[2] * frames[s + 2] + weights[3] * frames[s + 3]
        acc_ref[q, s * 8 : (s + 1) * 8, :] = total


def filter_fold(acc_ref, f_ref, column, block, inputs):
    for i in inputs:
        parts = [acc_ref[q, pl.ds(i, BLOCK, stride=8), :].astype(BF16) for q in range(4)]
        wide = [part.astype(F32) for part in parts]
        evens, odds = wide[0] + wide[2], wide[1] + wide[3]
        rows = pl.ds(pl.multiple_of((i % 4) * LANES + (i // 4) * HALF + block * BLOCK, BLOCK), BLOCK)
        f_ref[column, rows, :] = (evens + odds).astype(BF16)
        f_ref[4 + column, rows, :] = (evens - odds).astype(BF16)
        f_ref[8 + column, rows, :] = parts[0] - parts[2]
        f_ref[12 + column, rows, :] = parts[1] - parts[3]


def filter_block(frame_at, w_ref, accs, f_ref, block):
    for column in range(5):
        for q in range(4):
            if column < 4:
                filter_taps(frame_at, w_ref, accs[column % 2], column, q)
            if column > 0:
                filter_fold(accs[(column - 1) % 2], f_ref, column - 1, block, range(2 * q, 2 * q + 2))


def transform(f_ref, tables, results, out_ref, half):
    t0_ref, t1_ref, t2_ref = tables
    scale = 1.0 / (64.0 * math.sqrt(FRAME))
    tasks = [
        (t2_ref, 0, 8, results[0], 32, 32, 0),
        (t2_ref, 512, 8, results[1], 32, 32, 64),
        (t0_ref, 0, 0, results[2], 0, 16, 0),
        (t1_ref, 0, 4, results[3], 16, 16, 0),
    ]

    def multiply(task, pair):
        table, first_row, column, result = task[:4]
        right = [f_ref[column + c, pair * 256 : (pair + 1) * 256, :] for c in range(table.shape[1] // LANES)]
        left = table[first_row : first_row + 512, :]
        dims = (((1,), (1,)), ((), ()))
        sums = lax.dot_general(left, jnp.concatenate(right, axis=1), dims, preferred_element_type=F32) * scale
        for side in range(2):
            result[pl.ds(pair * 2 + side, 512, stride=4), :] = sums[:, side * LANES : (side + 1) * LANES]

    def emit(task, part):
        result, place, each, start = task[3:]
        place = place + half * 64
        count = 2048 // each // 2
        for d in range(part * count, (part + 1) * count, 4):
            rows = result[d * each : (d + 4) * each, :].astype(BF16)
            out_ref[start + d : start + d + 4, place : place + each, :] = rows.reshape(4, each, LANES)

    for n in range(len(tasks) + 1):
        for part in range(2):
            if n < len(tasks):
                multiply(tasks[n], part)
            if n > 0:
                emit(tasks[n - 1], part)


def late_kernel(spec_here, v_hbm, w_ref, f_ref, tail_ref, frames, acc_even, acc_odd, sems):
    begin = spec_here // 2 - (TAPS - 1)
    blocks = HALF // BLOCK

    def fetch(first, count, sem):
        rows = pl.ds(first, count)
        return pltpu.make_async_copy(v_hbm.at[pl.ds(begin + first, count)], frames.at[rows], sems.at[sem])

    fetch(0, TAPS - 1, blocks).start()
    for b in range(blocks):
        fetch(TAPS - 1 + b * BLOCK, BLOCK, b).start()
    fetch(0, TAPS - 1, blocks).wait()

    def step(b, carry):
        fetch(TAPS - 1 + b * BLOCK, BLOCK, b).wait()
        filter_block(lambda f, tile: frames[b * BLOCK + f, tile], w_ref, (acc_even, acc_odd), f_ref, b)
        return carry

    lax.fori_loop(0, blocks, step, 0)
    keep = jnp.where(lax.axis_index("ta") == lax.axis_size("ta") - 1, 0.0, 1.0).astype(F32)
    for f in range(TAPS - 1):
        tail_ref[f] = (frames[HALF + f].astype(F32) * keep).astype(BF16)


def middle_kernel(v_hbm, w_ref, late_ref, t0_ref, t1_ref, t2_ref, out_ref, f_ref, head_ref, frames, acc_even, acc_odd, sems, *results):
    begin = BLOCK - (TAPS - 1)
    blocks = HALF // BLOCK

    def fetch(first, count, sem):
        rows = pl.ds(first, count)
        return pltpu.make_async_copy(v_hbm.at[pl.ds(begin + first, count)], frames.at[rows], sems.at[sem])

    fetch(0, TAPS - 1, 0).start()
    for b in range(1, blocks):
        fetch(TAPS - 1 + (b - 1) * BLOCK, BLOCK, b).start()
    head = pltpu.make_async_copy(v_hbm.at[pl.ds(0, BLOCK)], head_ref, sems.at[blocks])
    head.start()
    transform(late_ref, (t0_ref, t1_ref, t2_ref), results, out_ref, 1)
    fetch(0, TAPS - 1, 0).wait()

    def step(b, carry):
        fetch(TAPS - 1 + (b - 1) * BLOCK, BLOCK, b).wait()
        filter_block(lambda f, tile: frames[(b - 1) * BLOCK + f, tile], w_ref, (acc_even, acc_odd), f_ref, b)
        return carry

    lax.fori_loop(1, blocks, step, 0)
    head.wait()


def early_kernel(head_ref, halo_ref, w_ref, t0_ref, t1_ref, t2_ref, f_in, out_in, out_ref, f_ref, acc_even, acc_odd, *results):
    def frame_at(f, tile):
        return halo_ref[f, tile] if f < TAPS - 1 else head_ref[f - (TAPS - 1), tile]

    filter_block(frame_at, w_ref, (acc_even, acc_odd), f_ref, 0)
    transform(f_ref, (t0_ref, t1_ref, t2_ref), results, out_ref, 0)


def gram_kernel(norm, got_ref, out_hbm, mats, out, sems):
    def copy_out(k, p):
        return pltpu.make_async_copy(out.at[k, p], out_hbm.at[k, p], sems.at[k, p])

    low = lax.broadcasted_iota(jnp.int32, (64, 8, LANES), 2) < HALF
    upper = lax.broadcasted_iota(jnp.int32, (64, 8, LANES), 1) < 4

    def sort(first, second):
        one = jnp.where(low, first, pltpu.roll(second, HALF, 2))
        two = jnp.where(low, pltpu.roll(first, HALF, 2), second)
        real = jnp.where(upper, one, pltpu.roll(two, 4, 1))
        imag = jnp.where(upper, pltpu.roll(one, 4, 1), two)
        return real.reshape(INPUTS, LANES).astype(BF16), imag.reshape(INPUTS, LANES).astype(BF16)

    for group, channels in enumerate(((0, 4), (2, 6), (1, 3), (5, 7))):
        for ta in range(2):
            halves = [got_ref[:, ta, h * 64 + group * 16 : h * 64 + (group + 1) * 16, :].astype(F32) for h in range(2)]
            for u in range(2):
                mat = mats.at[u]
                real, imag = sort(*[x[:, u * 8 : (u + 1) * 8, :] for x in halves])
                mat[:INPUTS, ta * 128 : (ta + 1) * 128] = real
                mat[:INPUTS, 256 + ta * 128 : 256 + (ta + 1) * 128] = imag
                mat[INPUTS:, ta * 128 : (ta + 1) * 128] = imag
                mat[INPUTS:, 256 + ta * 128 : 256 + (ta + 1) * 128] = -real
        for u, k in enumerate(channels):
            for p in range(2):
                left = mats[u, p * INPUTS : (p + 1) * INPUTS, :]
                dims = (((1,), (1,)), ((), ()))
                gram = lax.dot_general(left, mats[u, :INPUTS, :], dims, preferred_element_type=F32)
                out[k, p] = gram * norm
                copy_out(k, p).start()
    for k in range(8):
        for p in range(2):
            copy_out(k, p).wait()


VMEM = pl.BlockSpec(memory_space=pltpu.VMEM)
ANY = pl.BlockSpec(memory_space=pl.ANY)
FOLDED = jax.ShapeDtypeStruct((TILES, 8 * HALF, LANES), BF16)
PAYLOAD = jax.ShapeDtypeStruct((128, 128, LANES), BF16)
ACCS = [pltpu.VMEM((4, BLOCK * 8, LANES), F32)] * 2
RESULTS = [pltpu.VMEM((512 * 4, LANES), F32)] * 4


def late_call(frames, window):
    return pl.pallas_call(
        functools.partial(late_kernel, frames.shape[0]),
        out_shape=(FOLDED, jax.ShapeDtypeStruct((TAPS - 1, TILES, 8, LANES), BF16)),
        in_specs=[ANY, VMEM],
        out_specs=(VMEM, VMEM),
        scratch_shapes=[pltpu.VMEM((HALF + TAPS - 1, TILES, 8, LANES), jnp.int32)]
        + ACCS
        + [pltpu.SemaphoreType.DMA((HALF // BLOCK + 1,))],
        compiler_params=pltpu.CompilerParams(vmem_limit_bytes=46 * MIB),
        cost_estimate=pl.CostEstimate(flops=8 * 1024 * 1024, bytes_accessed=4 * MIB, transcendentals=0),
        name="late",
    )(frames, window)


def middle_call(frames, window, late, tables):
    return pl.pallas_call(
        middle_kernel,
        out_shape=(PAYLOAD, FOLDED, jax.ShapeDtypeStruct((BLOCK, TILES, 8, LANES), jnp.int32)),
        in_specs=[ANY] + [VMEM] * 5,
        out_specs=(VMEM, VMEM, VMEM),
        scratch_shapes=[pltpu.VMEM((HALF - BLOCK + TAPS - 1, TILES, 8, LANES), jnp.int32)]
        + ACCS
        + [pltpu.SemaphoreType.DMA((HALF // BLOCK + 1,))]
        + RESULTS,
        compiler_params=pltpu.CompilerParams(vmem_limit_bytes=40 * MIB),
        cost_estimate=pl.CostEstimate(flops=2 * 1024**3, bytes_accessed=12 * MIB, transcendentals=0),
        name="middle",
    )(frames, window, late, *tables)


def early_call(head, halo, window, tables, folded, payload):
    return pl.pallas_call(
        early_kernel,
        out_shape=(PAYLOAD, FOLDED),
        in_specs=[VMEM] * 8,
        out_specs=(VMEM, VMEM),
        input_output_aliases={6: 1, 7: 0},
        scratch_shapes=ACCS + RESULTS,
        compiler_params=pltpu.CompilerParams(vmem_limit_bytes=40 * MIB),
        cost_estimate=pl.CostEstimate(flops=2 * 1024**3, bytes_accessed=8 * MIB, transcendentals=0),
        name="early",
    )(head, halo, window, *tables, folded, payload)[0]


def gram_call(arrived, norm):
    return pl.pallas_call(
        lambda *refs: gram_kernel(norm, *refs),
        out_shape=jax.ShapeDtypeStruct((8, 2, INPUTS, INPUTS), F32),
        in_specs=[VMEM],
        out_specs=ANY,
        scratch_shapes=[
            pltpu.VMEM((2, 2 * INPUTS, 512), BF16),
            pltpu.VMEM((8, 2, INPUTS, INPUTS), F32),
            pltpu.SemaphoreType.DMA((8, 2)),
        ],
        compiler_params=pltpu.CompilerParams(vmem_limit_bytes=40 * MIB),
        cost_estimate=pl.CostEstimate(flops=4 * 1024**3, bytes_accessed=20 * MIB, transcendentals=0),
        name="gram",
    )(arrived)


def on_device(voltages):
    inputs_here, total_len = voltages.shape
    spec_here = total_len // FRAME
    frames = voltages.reshape(inputs_here, spec_here, TILES, LANES).transpose(1, 2, 0, 3)
    window = window_rows()
    tables = [jnp.asarray(dft_rows(0, 4, 512)), jnp.asarray(dft_rows(2, 4, 512)), jnp.asarray(dft_rows(1, 2, 1024))]
    late, tail = late_call(frames, window)
    halo = halo_of(tail)
    payload, folded, head = middle_call(frames, window, late, tables)
    outgoing = early_call(head, halo, window, tables, folded, payload)
    arrived = lax.all_to_all(outgoing, ("gx", "ta"), split_axis=0, concat_axis=0, tiled=True)
    norm = 1.0 / math.sqrt(2 * spec_here)
    return gram_call(arrived.reshape(64, 2, 128, spec_here), norm)


def solution(mesh):
    placed = (P("gx", "ta"),)
    return jax.shard_map(
        on_device,
        mesh=mesh,
        in_specs=placed,
        out_specs=P(("gx", "ta"), None, None, None),
        check_vma=False,
    )
```

```python
import functools
import math

import jax
import jax.numpy as jnp
import numpy as np
from jax import lax
from jax.experimental import pallas as pl
from jax.experimental.pallas import tpu as pltpu
from jax.sharding import PartitionSpec as P

INPUTS = 512
CHAN = 1024
TAPS = 4
FRAME = 2 * CHAN
LANES = 128
TILES = FRAME // LANES
BLOCK = 16
HALF = 64
MIB = 1024 * 1024
BF16 = jnp.bfloat16
F32 = jnp.float32


def halo_of(tail):
    count = lax.axis_size("ta")
    return lax.ppermute(tail, "ta", [(i, (i + 1) % count) for i in range(count)])


def window_rows():
    total_len = TAPS * FRAME
    tile = lax.broadcasted_iota(jnp.int32, (TAPS * TILES, LANES), 0)
    lane = lax.broadcasted_iota(jnp.int32, (TAPS * TILES, LANES), 1)
    positions = (tile * LANES + lane).astype(F32)
    centred = (positions + 0.5 - total_len / 2.0) / FRAME
    hamming = 0.54 - 0.46 * jnp.cos(2.0 * jnp.pi * positions / (total_len - 1))
    turn = jnp.pi * centred
    return jnp.sin(turn) / turn * hamming


def dft_rows(first, step, length):
    chan = np.arange(first, CHAN, step)
    phase = chan[:, None] * np.arange(length)[None, :] % FRAME
    angle = phase * (2.0 * np.pi / FRAME)
    rows = np.stack([np.cos(angle), -np.sin(angle)], axis=1)
    return rows.reshape(2 * chan.size, length).astype(BF16)


def filter_taps(frame_at, w_ref, acc_ref, column, q):
    tile = column + 4 * q
    weights = [jnp.broadcast_to(w_ref[pl.ds(t * TILES + tile, 1), :], (8, LANES)) for t in range(TAPS)]
    frames = [frame_at(f, tile).astype(F32) for f in range(BLOCK + TAPS - 1)]
    for s in range(BLOCK):
        total = weights[0] * frames[s] + weights[1] * frames[s + 1]
        total = total + weights[2] * frames[s + 2] + weights[3] * frames[s + 3]
        acc_ref[q, s * 8 : (s + 1) * 8, :] = total


def filter_fold(acc_ref, f_ref, column, block, inputs):
    for i in inputs:
        parts = [acc_ref[q, pl.ds(i, BLOCK, stride=8), :].astype(BF16) for q in range(4)]
        wide = [part.astype(F32) for part in parts]
        evens, odds = wide[0] + wide[2], wide[1] + wide[3]
        rows = pl.ds(pl.multiple_of((i % 4) * LANES + (i // 4) * HALF + block * BLOCK, BLOCK), BLOCK)
        f_ref[column, rows, :] = (evens + odds).astype(BF16)
        f_ref[4 + column, rows, :] = (evens - odds).astype(BF16)
        f_ref[8 + column, rows, :] = parts[0] - parts[2]
        f_ref[12 + column, rows, :] = parts[1] - parts[3]


def filter_block(frame_at, w_ref, accs, f_ref, block):
    for column in range(5):
        for q in range(4):
            if column < 4:
                filter_taps(frame_at, w_ref, accs[column % 2], column, q)
            if column > 0:
                filter_fold(accs[(column - 1) % 2], f_ref, column - 1, block, range(2 * q, 2 * q + 2))


def transform(f_ref, tables, results, out_ref, half):
    t0_ref, t1_ref, t2_ref = tables
    scale = 1.0 / (64.0 * math.sqrt(FRAME))
    tasks = [
        (t2_ref, 0, 8, results[0], 32, 32, 0),
        (t2_ref, 512, 8, results[1], 32, 32, 64),
        (t0_ref, 0, 0, results[2], 0, 16, 0),
        (t1_ref, 0, 4, results[3], 16, 16, 0),
    ]

    def multiply(task, pair):
        table, first_row, column, result = task[:4]
        right = [f_ref[column + c, pair * 256 : (pair + 1) * 256, :] for c in range(table.shape[1] // LANES)]
        left = table[first_row : first_row + 512, :]
        dims = (((1,), (1,)), ((), ()))
        sums = lax.dot_general(left, jnp.concatenate(right, axis=1), dims, preferred_element_type=F32) * scale
        for side in range(2):
            result[pl.ds(pair * 2 + side, 512, stride=4), :] = sums[:, side * LANES : (side + 1) * LANES]

    def emit(task, part):
        result, place, each, start = task[3:]
        place = place + half * 64
        count = 2048 // each // 2
        for d in range(part * count, (part + 1) * count, 4):
            rows = result[d * each : (d + 4) * each, :].astype(BF16)
            out_ref[start + d : start + d + 4, place : place + each, :] = rows.reshape(4, each, LANES)

    for n in range(len(tasks) + 1):
        for part in range(2):
            if n < len(tasks):
                multiply(tasks[n], part)
            if n > 0:
                emit(tasks[n - 1], part)


def late_kernel(spec_here, v_hbm, f_ref, tail_ref, w_ref, frames, acc_even, acc_odd, sems):
    begin = spec_here // 2 - (TAPS - 1)
    blocks = HALF // BLOCK

    def fetch(first, count, sem):
        rows = pl.ds(first, count)
        return pltpu.make_async_copy(v_hbm.at[pl.ds(begin + first, count)], frames.at[rows], sems.at[sem])

    fetch(0, TAPS - 1, blocks).start()
    for b in range(blocks):
        fetch(TAPS - 1 + b * BLOCK, BLOCK, b).start()
    w_ref[...] = window_rows()
    fetch(0, TAPS - 1, blocks).wait()

    def step(b, carry):
        fetch(TAPS - 1 + b * BLOCK, BLOCK, b).wait()
        filter_block(lambda f, tile: frames[b * BLOCK + f, tile], w_ref, (acc_even, acc_odd), f_ref, b)
        return carry

    lax.fori_loop(0, blocks, step, 0)
    keep = jnp.where(lax.axis_index("ta") == lax.axis_size("ta") - 1, 0.0, 1.0).astype(F32)
    for f in range(TAPS - 1):
        tail_ref[f] = (frames[HALF + f].astype(F32) * keep).astype(BF16)


def middle_kernel(v_hbm, w_ref, late_ref, t0_ref, t1_ref, t2_ref, out_ref, f_ref, head_ref, frames, acc_even, acc_odd, sems, *results):
    begin = BLOCK - (TAPS - 1)
    blocks = HALF // BLOCK

    def fetch(first, count, sem):
        rows = pl.ds(first, count)
        return pltpu.make_async_copy(v_hbm.at[pl.ds(begin + first, count)], frames.at[rows], sems.at[sem])

    fetch(0, TAPS - 1, 0).start()
    for b in range(1, blocks):
        fetch(TAPS - 1 + (b - 1) * BLOCK, BLOCK, b).start()
    head = pltpu.make_async_copy(v_hbm.at[pl.ds(0, BLOCK)], head_ref, sems.at[blocks])
    head.start()
    transform(late_ref, (t0_ref, t1_ref, t2_ref), results, out_ref, 1)
    fetch(0, TAPS - 1, 0).wait()

    def step(b, carry):
        fetch(TAPS - 1 + (b - 1) * BLOCK, BLOCK, b).wait()
        filter_block(lambda f, tile: frames[(b - 1) * BLOCK + f, tile], w_ref, (acc_even, acc_odd), f_ref, b)
        return carry

    lax.fori_loop(1, blocks, step, 0)
    head.wait()


def early_kernel(head_ref, halo_ref, w_ref, t0_ref, t1_ref, t2_ref, f_in, out_in, out_ref, f_ref, acc_even, acc_odd, *results):
    def frame_at(f, tile):
        return halo_ref[f, tile] if f < TAPS - 1 else head_ref[f - (TAPS - 1), tile]

    filter_block(frame_at, w_ref, (acc_even, acc_odd), f_ref, 0)
    transform(f_ref, (t0_ref, t1_ref, t2_ref), results, out_ref, 0)


def gram_kernel(norm, got_ref, out_hbm, mats, out, sems):
    def copy_out(k, p):
        return pltpu.make_async_copy(out.at[k, p], out_hbm.at[k, p], sems.at[k, p])

    low = lax.broadcasted_iota(jnp.int32, (64, 8, LANES), 2) < HALF
    upper = lax.broadcasted_iota(jnp.int32, (64, 8, LANES), 1) < 4

    def sort(first, second):
        one = jnp.where(low, first, pltpu.roll(second, HALF, 2))
        two = jnp.where(low, pltpu.roll(first, HALF, 2), second)
        real = jnp.where(upper, one, pltpu.roll(two, 4, 1))
        imag = jnp.where(upper, pltpu.roll(one, 4, 1), two)
        return real.reshape(INPUTS, LANES).astype(BF16), imag.reshape(INPUTS, LANES).astype(BF16)

    for group, channels in enumerate(((0, 4), (2, 6), (1, 3), (5, 7))):
        for u, k in enumerate(channels):
            mat = mats.at[u]
            for ta in range(2):
                rows = [slice(h * 64 + group * 16, h * 64 + (group + 1) * 16) for h in range(2)]
                halves = [got_ref[:, ta, part, :].astype(F32)[:, u * 8 : (u + 1) * 8, :] for part in rows]
                real, imag = sort(*halves)
                mat[:INPUTS, ta * 128 : (ta + 1) * 128] = real
                mat[:INPUTS, 256 + ta * 128 : 256 + (ta + 1) * 128] = imag
                mat[INPUTS:, ta * 128 : (ta + 1) * 128] = imag
                mat[INPUTS:, 256 + ta * 128 : 256 + (ta + 1) * 128] = -real
            for p in range(2):
                left = mats[u, p * INPUTS : (p + 1) * INPUTS, :]
                dims = (((1,), (1,)), ((), ()))
                gram = lax.dot_general(left, mats[u, :INPUTS, :], dims, preferred_element_type=F32)
                out[k, p] = gram * norm
                copy_out(k, p).start()
    for k in range(8):
        for p in range(2):
            copy_out(k, p).wait()


VMEM = pl.BlockSpec(memory_space=pltpu.VMEM)
ANY = pl.BlockSpec(memory_space=pl.ANY)
FOLDED = jax.ShapeDtypeStruct((TILES, 8 * HALF, LANES), BF16)
PAYLOAD = jax.ShapeDtypeStruct((128, 128, LANES), BF16)
ACCS = [pltpu.VMEM((4, BLOCK * 8, LANES), F32)] * 2
RESULTS = [pltpu.VMEM((512 * 4, LANES), F32)] * 4


def late_call(frames):
    return pl.pallas_call(
        functools.partial(late_kernel, frames.shape[0]),
        out_shape=(
            FOLDED,
            jax.ShapeDtypeStruct((TAPS - 1, TILES, 8, LANES), BF16),
            jax.ShapeDtypeStruct((TAPS * TILES, LANES), F32),
        ),
        in_specs=[ANY],
        out_specs=(VMEM, VMEM, VMEM),
        scratch_shapes=[pltpu.VMEM((HALF + TAPS - 1, TILES, 8, LANES), jnp.int32)]
        + ACCS
        + [pltpu.SemaphoreType.DMA((HALF // BLOCK + 1,))],
        compiler_params=pltpu.CompilerParams(vmem_limit_bytes=46 * MIB),
        cost_estimate=pl.CostEstimate(flops=8 * 1024 * 1024, bytes_accessed=4 * MIB, transcendentals=0),
        name="late",
    )(frames)


def middle_call(frames, window, late, tables):
    return pl.pallas_call(
        middle_kernel,
        out_shape=(PAYLOAD, FOLDED, jax.ShapeDtypeStruct((BLOCK, TILES, 8, LANES), jnp.int32)),
        in_specs=[ANY] + [VMEM] * 5,
        out_specs=(VMEM, VMEM, VMEM),
        scratch_shapes=[pltpu.VMEM((HALF - BLOCK + TAPS - 1, TILES, 8, LANES), jnp.int32)]
        + ACCS
        + [pltpu.SemaphoreType.DMA((HALF // BLOCK + 1,))]
        + RESULTS,
        compiler_params=pltpu.CompilerParams(vmem_limit_bytes=40 * MIB),
        cost_estimate=pl.CostEstimate(flops=2 * 1024**3, bytes_accessed=12 * MIB, transcendentals=0),
        name="middle",
    )(frames, window, late, *tables)


def early_call(head, halo, window, tables, folded, payload):
    return pl.pallas_call(
        early_kernel,
        out_shape=(PAYLOAD, FOLDED),
        in_specs=[VMEM] * 8,
        out_specs=(VMEM, VMEM),
        input_output_aliases={6: 1, 7: 0},
        scratch_shapes=ACCS + RESULTS,
        compiler_params=pltpu.CompilerParams(vmem_limit_bytes=40 * MIB),
        cost_estimate=pl.CostEstimate(flops=2 * 1024**3, bytes_accessed=8 * MIB, transcendentals=0),
        name="early",
    )(head, halo, window, *tables, folded, payload)[0]


def gram_call(arrived, norm):
    return pl.pallas_call(
        lambda *refs: gram_kernel(norm, *refs),
        out_shape=jax.ShapeDtypeStruct((8, 2, INPUTS, INPUTS), F32),
        in_specs=[VMEM],
        out_specs=ANY,
        scratch_shapes=[
            pltpu.VMEM((2, 2 * INPUTS, 512), BF16),
            pltpu.VMEM((8, 2, INPUTS, INPUTS), F32),
            pltpu.SemaphoreType.DMA((8, 2)),
        ],
        compiler_params=pltpu.CompilerParams(vmem_limit_bytes=40 * MIB),
        cost_estimate=pl.CostEstimate(flops=4 * 1024**3, bytes_accessed=20 * MIB, transcendentals=0),
        name="gram",
    )(arrived)


def on_device(voltages):
    inputs_here, total_len = voltages.shape
    spec_here = total_len // FRAME
    frames = voltages.reshape(inputs_here, spec_here, TILES, LANES).transpose(1, 2, 0, 3)
    tables = [jnp.asarray(dft_rows(0, 4, 512)), jnp.asarray(dft_rows(2, 4, 512)), jnp.asarray(dft_rows(1, 2, 1024))]
    late, tail, window = late_call(frames)
    halo = halo_of(tail)
    payload, folded, head = middle_call(frames, window, late, tables)
    outgoing = early_call(head, halo, window, tables, folded, payload)
    arrived = lax.all_to_all(outgoing, ("gx", "ta"), split_axis=0, concat_axis=0, tiled=True)
    norm = 1.0 / math.sqrt(2 * spec_here)
    return gram_call(arrived.reshape(64, 2, 128, spec_here), norm)


def solution(mesh):
    placed = (P("gx", "ta"),)
    return jax.shard_map(
        on_device,
        mesh=mesh,
        in_specs=placed,
        out_specs=P(("gx", "ta"), None, None, None),
        check_vma=False,
    )
```

```python
import functools
import math

import jax
import jax.numpy as jnp
import numpy as np
from jax import lax
from jax.experimental import pallas as pl
from jax.experimental.pallas import tpu as pltpu
from jax.sharding import PartitionSpec as P

INPUTS = 512
CHAN = 1024
TAPS = 4
FRAME = 2 * CHAN
LANES = 128
TILES = FRAME // LANES
BLOCK = 16
HALF = 64
MIB = 1024 * 1024
BF16 = jnp.bfloat16
F32 = jnp.float32


def halo_of(tail):
    count = lax.axis_size("ta")
    return lax.ppermute(tail, "ta", [(i, (i + 1) % count) for i in range(count)])


def window_rows():
    total_len = TAPS * FRAME
    tile = lax.broadcasted_iota(jnp.int32, (TAPS * TILES, LANES), 0)
    lane = lax.broadcasted_iota(jnp.int32, (TAPS * TILES, LANES), 1)
    positions = (tile * LANES + lane).astype(F32)
    centred = (positions + 0.5 - total_len / 2.0) / FRAME
    hamming = 0.54 - 0.46 * jnp.cos(2.0 * jnp.pi * positions / (total_len - 1))
    turn = jnp.pi * centred
    return jnp.sin(turn) / turn * hamming


def dft_rows(first, step, length):
    chan = np.arange(first, CHAN, step)
    phase = chan[:, None] * np.arange(length)[None, :] % FRAME
    angle = phase * (2.0 * np.pi / FRAME)
    rows = np.stack([np.cos(angle), -np.sin(angle)], axis=1)
    return rows.reshape(2 * chan.size, length).astype(BF16)


def filter_taps(frame_at, w_ref, acc_ref, column, q):
    tile = column + 4 * q
    weights = [jnp.broadcast_to(w_ref[pl.ds(t * TILES + tile, 1), :], (8, LANES)) for t in range(TAPS)]
    frames = [frame_at(f, tile).astype(F32) for f in range(BLOCK + TAPS - 1)]
    for s in range(BLOCK):
        total = weights[0] * frames[s] + weights[1] * frames[s + 1]
        total = total + weights[2] * frames[s + 2] + weights[3] * frames[s + 3]
        acc_ref[q, s * 8 : (s + 1) * 8, :] = total


def filter_fold(acc_ref, f_ref, column, block, inputs):
    for i in inputs:
        parts = [acc_ref[q, pl.ds(i, BLOCK, stride=8), :].astype(BF16) for q in range(4)]
        wide = [part.astype(F32) for part in parts]
        evens, odds = wide[0] + wide[2], wide[1] + wide[3]
        rows = pl.ds(pl.multiple_of((i % 4) * LANES + (i // 4) * HALF + block * BLOCK, BLOCK), BLOCK)
        f_ref[column, rows, :] = (evens + odds).astype(BF16)
        f_ref[4 + column, rows, :] = (evens - odds).astype(BF16)
        f_ref[8 + column, rows, :] = parts[0] - parts[2]
        f_ref[12 + column, rows, :] = parts[1] - parts[3]


def filter_block(frame_at, w_ref, accs, f_ref, block):
    for column in range(5):
        for q in range(4):
            if column < 4:
                filter_taps(frame_at, w_ref, accs[column % 2], column, q)
            if column > 0:
                filter_fold(accs[(column - 1) % 2], f_ref, column - 1, block, range(2 * q, 2 * q + 2))


def transform(f_ref, tables, results, out_ref, half):
    t0_ref, t1_ref, t2_ref = tables
    scale = 1.0 / (64.0 * math.sqrt(FRAME))
    tasks = [
        (t2_ref, 0, 8, results[0], 32, 32, 0),
        (t2_ref, 512, 8, results[1], 32, 32, 64),
        (t0_ref, 0, 0, results[2], 0, 16, 0),
        (t1_ref, 0, 4, results[3], 16, 16, 0),
    ]

    def multiply(task, pair):
        table, first_row, column, result = task[:4]
        right = [f_ref[column + c, pair * 256 : (pair + 1) * 256, :] for c in range(table.shape[1] // LANES)]
        left = table[first_row : first_row + 512, :]
        dims = (((1,), (1,)), ((), ()))
        sums = lax.dot_general(left, jnp.concatenate(right, axis=1), dims, preferred_element_type=F32) * scale
        for side in range(2):
            result[pl.ds(pair * 2 + side, 512, stride=4), :] = sums[:, side * LANES : (side + 1) * LANES]

    def emit(task, part):
        result, place, each, start = task[3:]
        place = place + half * 64
        count = 2048 // each // 2
        for d in range(part * count, (part + 1) * count, 4):
            rows = result[d * each : (d + 4) * each, :].astype(BF16)
            out_ref[start + d : start + d + 4, place : place + each, :] = rows.reshape(4, each, LANES)

    for n in range(len(tasks) + 1):
        for part in range(2):
            if n < len(tasks):
                multiply(tasks[n], part)
            if n > 0:
                emit(tasks[n - 1], part)


def late_kernel(spec_here, v_hbm, f_ref, tail_ref, w_ref, frames, acc_even, acc_odd, sems):
    begin = spec_here // 2 - (TAPS - 1)
    blocks = HALF // BLOCK

    def fetch(first, count, sem):
        rows = pl.ds(first, count)
        return pltpu.make_async_copy(v_hbm.at[pl.ds(begin + first, count)], frames.at[rows], sems.at[sem])

    fetch(0, TAPS - 1, blocks).start()
    for b in range(blocks):
        fetch(TAPS - 1 + b * BLOCK, BLOCK, b).start()
    w_ref[...] = window_rows()
    fetch(0, TAPS - 1, blocks).wait()

    def step(b, carry):
        fetch(TAPS - 1 + b * BLOCK, BLOCK, b).wait()
        filter_block(lambda f, tile: frames[b * BLOCK + f, tile], w_ref, (acc_even, acc_odd), f_ref, b)
        return carry

    lax.fori_loop(0, blocks, step, 0, unroll=True)
    keep = jnp.where(lax.axis_index("ta") == lax.axis_size("ta") - 1, 0.0, 1.0).astype(F32)
    for f in range(TAPS - 1):
        tail_ref[f] = (frames[HALF + f].astype(F32) * keep).astype(BF16)


def middle_kernel(v_hbm, w_ref, late_ref, t0_ref, t1_ref, t2_ref, out_ref, f_ref, head_ref, frames, acc_even, acc_odd, sems, *results):
    begin = BLOCK - (TAPS - 1)
    blocks = HALF // BLOCK

    def fetch(first, count, sem):
        rows = pl.ds(first, count)
        return pltpu.make_async_copy(v_hbm.at[pl.ds(begin + first, count)], frames.at[rows], sems.at[sem])

    fetch(0, TAPS - 1, 0).start()
    for b in range(1, blocks):
        fetch(TAPS - 1 + (b - 1) * BLOCK, BLOCK, b).start()
    head = pltpu.make_async_copy(v_hbm.at[pl.ds(0, BLOCK)], head_ref, sems.at[blocks])
    head.start()
    transform(late_ref, (t0_ref, t1_ref, t2_ref), results, out_ref, 1)
    fetch(0, TAPS - 1, 0).wait()

    def step(b, carry):
        fetch(TAPS - 1 + (b - 1) * BLOCK, BLOCK, b).wait()
        filter_block(lambda f, tile: frames[(b - 1) * BLOCK + f, tile], w_ref, (acc_even, acc_odd), f_ref, b)
        return carry

    lax.fori_loop(1, blocks, step, 0, unroll=True)
    head.wait()


def early_kernel(head_ref, halo_ref, w_ref, t0_ref, t1_ref, t2_ref, f_in, out_in, out_ref, f_ref, acc_even, acc_odd, *results):
    def frame_at(f, tile):
        return halo_ref[f, tile] if f < TAPS - 1 else head_ref[f - (TAPS - 1), tile]

    filter_block(frame_at, w_ref, (acc_even, acc_odd), f_ref, 0)
    transform(f_ref, (t0_ref, t1_ref, t2_ref), results, out_ref, 0)


def gram_kernel(norm, got_ref, out_hbm, mats, out, sems):
    def copy_out(k, p):
        return pltpu.make_async_copy(out.at[k, p], out_hbm.at[k, p], sems.at[k, p])

    low = lax.broadcasted_iota(jnp.int32, (64, 8, LANES), 2) < HALF
    upper = lax.broadcasted_iota(jnp.int32, (64, 8, LANES), 1) < 4

    def sort(first, second):
        one = jnp.where(low, first, pltpu.roll(second, HALF, 2))
        two = jnp.where(low, pltpu.roll(first, HALF, 2), second)
        real = jnp.where(upper, one, pltpu.roll(two, 4, 1))
        imag = jnp.where(upper, pltpu.roll(one, 4, 1), two)
        return real.reshape(INPUTS, LANES).astype(BF16), imag.reshape(INPUTS, LANES).astype(BF16)

    for group, channels in enumerate(((0, 4), (2, 6), (1, 3), (5, 7))):
        for u, k in enumerate(channels):
            mat = mats.at[u]
            for ta in range(2):
                rows = [slice(h * 64 + group * 16, h * 64 + (group + 1) * 16) for h in range(2)]
                halves = [got_ref[:, ta, part, :].astype(F32)[:, u * 8 : (u + 1) * 8, :] for part in rows]
                real, imag = sort(*halves)
                mat[:INPUTS, ta * 128 : (ta + 1) * 128] = real
                mat[:INPUTS, 256 + ta * 128 : 256 + (ta + 1) * 128] = imag
                mat[INPUTS:, ta * 128 : (ta + 1) * 128] = imag
                mat[INPUTS:, 256 + ta * 128 : 256 + (ta + 1) * 128] = -real
            for p in range(2):
                left = mats[u, p * INPUTS : (p + 1) * INPUTS, :]
                dims = (((1,), (1,)), ((), ()))
                gram = lax.dot_general(left, mats[u, :INPUTS, :], dims, preferred_element_type=F32)
                out[k, p] = gram * norm
                copy_out(k, p).start()
    for k in range(8):
        for p in range(2):
            copy_out(k, p).wait()


VMEM = pl.BlockSpec(memory_space=pltpu.VMEM)
ANY = pl.BlockSpec(memory_space=pl.ANY)
FOLDED = jax.ShapeDtypeStruct((TILES, 8 * HALF, LANES), BF16)
PAYLOAD = jax.ShapeDtypeStruct((128, 128, LANES), BF16)
ACCS = [pltpu.VMEM((4, BLOCK * 8, LANES), F32)] * 2
RESULTS = [pltpu.VMEM((512 * 4, LANES), F32)] * 4


def late_call(frames):
    return pl.pallas_call(
        functools.partial(late_kernel, frames.shape[0]),
        out_shape=(
            FOLDED,
            jax.ShapeDtypeStruct((TAPS - 1, TILES, 8, LANES), BF16),
            jax.ShapeDtypeStruct((TAPS * TILES, LANES), F32),
        ),
        in_specs=[ANY],
        out_specs=(VMEM, VMEM, VMEM),
        scratch_shapes=[pltpu.VMEM((HALF + TAPS - 1, TILES, 8, LANES), jnp.int32)]
        + ACCS
        + [pltpu.SemaphoreType.DMA((HALF // BLOCK + 1,))],
        compiler_params=pltpu.CompilerParams(vmem_limit_bytes=46 * MIB),
        cost_estimate=pl.CostEstimate(flops=8 * 1024 * 1024, bytes_accessed=4 * MIB, transcendentals=0),
        name="late",
    )(frames)


def middle_call(frames, window, late, tables):
    return pl.pallas_call(
        middle_kernel,
        out_shape=(PAYLOAD, FOLDED, jax.ShapeDtypeStruct((BLOCK, TILES, 8, LANES), jnp.int32)),
        in_specs=[ANY] + [VMEM] * 5,
        out_specs=(VMEM, VMEM, VMEM),
        scratch_shapes=[pltpu.VMEM((HALF - BLOCK + TAPS - 1, TILES, 8, LANES), jnp.int32)]
        + ACCS
        + [pltpu.SemaphoreType.DMA((HALF // BLOCK + 1,))]
        + RESULTS,
        compiler_params=pltpu.CompilerParams(vmem_limit_bytes=40 * MIB),
        cost_estimate=pl.CostEstimate(flops=2 * 1024**3, bytes_accessed=12 * MIB, transcendentals=0),
        name="middle",
    )(frames, window, late, *tables)


def early_call(head, halo, window, tables, folded, payload):
    return pl.pallas_call(
        early_kernel,
        out_shape=(PAYLOAD, FOLDED),
        in_specs=[VMEM] * 8,
        out_specs=(VMEM, VMEM),
        input_output_aliases={6: 1, 7: 0},
        scratch_shapes=ACCS + RESULTS,
        compiler_params=pltpu.CompilerParams(vmem_limit_bytes=40 * MIB),
        cost_estimate=pl.CostEstimate(flops=2 * 1024**3, bytes_accessed=8 * MIB, transcendentals=0),
        name="early",
    )(head, halo, window, *tables, folded, payload)[0]


def gram_call(arrived, norm):
    return pl.pallas_call(
        lambda *refs: gram_kernel(norm, *refs),
        out_shape=jax.ShapeDtypeStruct((8, 2, INPUTS, INPUTS), F32),
        in_specs=[VMEM],
        out_specs=ANY,
        scratch_shapes=[
            pltpu.VMEM((2, 2 * INPUTS, 512), BF16),
            pltpu.VMEM((8, 2, INPUTS, INPUTS), F32),
            pltpu.SemaphoreType.DMA((8, 2)),
        ],
        compiler_params=pltpu.CompilerParams(vmem_limit_bytes=40 * MIB),
        cost_estimate=pl.CostEstimate(flops=4 * 1024**3, bytes_accessed=20 * MIB, transcendentals=0),
        name="gram",
    )(arrived)


def on_device(voltages):
    inputs_here, total_len = voltages.shape
    spec_here = total_len // FRAME
    frames = voltages.reshape(inputs_here, spec_here, TILES, LANES).transpose(1, 2, 0, 3)
    tables = [jnp.asarray(dft_rows(0, 4, 512)), jnp.asarray(dft_rows(2, 4, 512)), jnp.asarray(dft_rows(1, 2, 1024))]
    late, tail, window = late_call(frames)
    halo = halo_of(tail)
    payload, folded, head = middle_call(frames, window, late, tables)
    outgoing = early_call(head, halo, window, tables, folded, payload)
    arrived = lax.all_to_all(outgoing, ("gx", "ta"), split_axis=0, concat_axis=0, tiled=True)
    norm = 1.0 / math.sqrt(2 * spec_here)
    return gram_call(arrived.reshape(64, 2, 128, spec_here), norm)


def solution(mesh):
    placed = (P("gx", "ta"),)
    return jax.shard_map(
        on_device,
        mesh=mesh,
        in_specs=placed,
        out_specs=P(("gx", "ta"), None, None, None),
        check_vma=False,
    )
```
